128 devices in a mesh: row: 8 (over x, core), col: 16 (over z, y).
Axes of the slice: x: 4, y: 4, z: 4, core: 2. Of those that a mesh axis runs over, the one named last changes fastest.
Arguments:
- features: bfloat16 [2, 16384, 256], P(None, ('row', 'col')), may hold values from -6 to 6
- adjacency: bfloat16 [8, 16, 512, 128, 128], P('row', 'col'), may hold values from -0.09375 to 0.09375
- requests: int32 [8, 16, 16, 2], P('row', 'col'), may hold values from -1 to 15, as said below
- block_coords: int32 [8, 16, 512, 2], P('row', 'col'), may hold values from 0 to 31, as said below
- weight: bfloat16 [256, 256], replicated, may hold values from -0.375 to 0.375
- cotangent: bfloat16 [262144, 256], P(('row', 'col')), may hold values from -6 to 6
Outputs:
- activations: bfloat16 [262144, 256], P(('row', 'col'))
- weight_grad: float32 [256, 256], replicated
- feature_grad: bfloat16 [2, 16384, 256], P(None, ('row', 'col'))
The draws below stay inside these ranges and needn't reach their ends.
Inputs may be any that keep to these rules, and one draw needn't show every extreme that they name: `requests`: -1 marks an unused entry; a used entry is a block of grid column s counted over the two panels, panel first, then grid row, then block. For each (r, c, s) the used entries come first and are distinct, and each device (r, c) uses all 2 entries for at least one column s. `block_coords`: the first coordinate is an output block of the device. The second is a receive slot s * 2 + j whose entry requests[r, c, s, j] of the same device is used; every used entry is named by at least one nonzero.
All inputs are finite; a program needn't handle non-finite values.
Results may differ from the reference program's by a relative error of at most 0.0063.
Values may be sent and summed in bfloat16 or wider, within the bound.
No kernel may reach another device: no remote copies, remote signals or barrier semaphores. Data moves between devices by JAX's collectives and lax.ppermute only.
A program may use at most 192 MiB of HBM per device.

```python
import jax
import jax.numpy as jnp
from jax import lax

F = 256
BLK = 128
OB = 16
SB = 1
LIST = 2
NNZ = 512
OUT_ROWS = 262144
PANEL = 16384
N_ROW = 8
N_COL = 16


def needed_lists(key):
    keys = jax.random.split(key, 5)
    group = 2 * N_ROW * SB
    counts = jax.random.randint(keys[0], (N_ROW, N_COL, N_COL), 1, LIST + 1)
    full_peer = jax.random.randint(keys[1], (N_ROW, N_COL), 0, N_COL)
    counts = jnp.where(jnp.arange(N_COL)[None, None, :] == full_peer[:, :, None], LIST, counts)
    scores = jax.random.randint(keys[2], (N_ROW, N_COL, N_COL, group), 0, 1 << 20)
    order = jnp.argsort(scores, axis=-1)[..., :LIST]
    live = jnp.arange(LIST)[None, None, None, :] < counts[..., None]
    wanted = jnp.where(live, order, -1).astype(jnp.int32)
    live_flat = live.reshape(N_ROW, N_COL, N_COL * LIST)
    live_count = jnp.sum(counts, axis=-1)
    slot_order = jnp.argsort(jnp.where(live_flat, 0, 1), axis=-1)
    extra = jax.random.randint(keys[3], (N_ROW, N_COL, NNZ), 0, 1 << 20) % live_count[..., None]
    position = jnp.arange(NNZ)[None, None, :]
    chosen = jnp.where(position < live_count[..., None], position, extra)
    slots = jnp.take_along_axis(slot_order, chosen, axis=-1)
    out_rows = jax.random.randint(keys[4], (N_ROW, N_COL, NNZ), 0, OB)
    coords = jnp.stack([out_rows, slots], axis=-1).astype(jnp.int32)
    return (wanted, coords)


def draw_requests(key, part):
    wanted, coords = needed_lists(key)
    return wanted


def draw_block_coords(key, part):
    wanted, coords = needed_lists(key)
    return coords


def levels(own_key, dims, shards, least, largest):
    level, own = 1.0, jax.random.fold_in(own_key, 6)
    for axis_at, blocks in shards:
        draws = jnp.exp(jax.random.uniform(jax.random.fold_in(own, axis_at), (blocks,), jnp.float32, least / len(shards), largest / len(shards)))
        level = level * jnp.repeat(draws, dims[axis_at] // blocks).reshape([-1 if axis == axis_at else 1 for axis in range(len(dims))])
    return level


def gaussian(stream_key, extent, scale, bound, pieces=(), dtype=jnp.bfloat16):
    gain = levels(stream_key, extent, pieces, -0.22, 0.18) if pieces else 1.0
    values = jax.random.normal(stream_key, extent, jnp.float32) * scale * gain
    return jnp.minimum(jnp.maximum(values, -bound), bound).astype(dtype)


def setup_inputs(seed: int = 0) -> dict:
    key_list = jax.random.split(jax.random.key(seed), 7)
    features = gaussian(key_list[0], (2, PANEL, F), 1.0, 6.0, ((1, 128),))
    adjacency = gaussian(key_list[1], (N_ROW, N_COL, NNZ, BLK, BLK), (BLK * NNZ // OB) ** -0.5, 0.09375, ((0, 8), (1, 16)))
    requests = draw_requests(jax.random.fold_in(key_list[6], 71), 0)
    block_coords = draw_block_coords(jax.random.fold_in(key_list[6], 71), 0)
    weight = gaussian(key_list[4], (F, F), F ** -0.5, 0.375)
    cotangent = gaussian(key_list[5], (OUT_ROWS, F), 1.0, 6.0, ((0, 128),))
    return {"features": features, "adjacency": adjacency, "requests": requests, "block_coords": block_coords, "weight": weight, "cotangent": cotangent}


def reference(features, adjacency, requests, block_coords, weight, cotangent):
    per_group = N_ROW * SB
    panel_blocks = N_ROW * N_COL * SB
    blocks = features.reshape(2 * panel_blocks, BLK, F)
    edges_all = adjacency.reshape(N_ROW * N_COL, NNZ, BLK, BLK)
    wanted_all = requests.reshape(N_ROW * N_COL, N_COL, LIST)
    coords_all = block_coords.reshape(N_ROW * N_COL, NNZ, 2)
    cot_all = cotangent.reshape(N_ROW * N_COL, OB * BLK, F)

    def one_device(carry, item):
        weight_sum, grad_sum = carry
        edges, wanted, coords, cot = item
        out_block = coords[:, 0].astype(jnp.int32)
        slot = coords[:, 1].astype(jnp.int32)
        source_col = slot // LIST
        entry = slot % LIST
        picked = wanted[source_col, entry].astype(jnp.int32)
        panel = picked // per_group
        within = picked % per_group
        source_block = (panel * panel_blocks + (within // SB * N_COL + source_col) * SB + within % SB).astype(jnp.int32)
        edge_vals = edges.astype(jnp.float32)
        source_rows = blocks[source_block].astype(jnp.float32)
        products = jnp.einsum('nij,njf->nif', edge_vals, source_rows, precision=lax.Precision.HIGHEST)
        aggregated = jax.ops.segment_sum(products, out_block, OB).astype(jnp.bfloat16).reshape(OB * BLK, F)
        pre = jnp.dot(aggregated, weight, preferred_element_type=jnp.float32)
        activ, pull = jax.vjp(jax.nn.gelu, pre)
        pre_grad = pull(cot.astype(jnp.float32))[0].astype(jnp.bfloat16)
        weight_sum = weight_sum + jnp.dot(aggregated.T, pre_grad, preferred_element_type=jnp.float32)
        row_grad = jnp.dot(pre_grad, weight.T, preferred_element_type=jnp.float32).astype(jnp.bfloat16).reshape(OB, BLK, F)
        contrib = jnp.einsum('nji,njf->nif', edge_vals, row_grad[out_block].astype(jnp.float32), precision=lax.Precision.HIGHEST)
        grad_sum = grad_sum.at[source_block].add(contrib)
        return ((weight_sum, grad_sum), activ.astype(jnp.bfloat16))
    start = (jnp.zeros((F, F), jnp.float32), jnp.zeros((2 * panel_blocks, BLK, F), jnp.float32))
    (weight_sum, grad_sum), activs = lax.scan(one_device, start, (edges_all, wanted_all, coords_all, cot_all))
    return (activs.reshape(OUT_ROWS, F), weight_sum, grad_sum.reshape(2, PANEL, F).astype(jnp.bfloat16))
```

```python
import functools
import math

import jax
import jax.numpy as jnp
from jax import lax
from jax.experimental import pallas as pl
from jax.experimental.pallas import tpu as pltpu
from jax.sharding import PartitionSpec as P

GELU_SCALE = math.sqrt(2 / math.pi)
GELU_CUBE = 0.044715
SMEM = pl.BlockSpec(memory_space=pltpu.SMEM)
VMEM = pl.BlockSpec(memory_space=pltpu.VMEM)
ANY = pl.BlockSpec(memory_space=pl.ANY)


def block(index, size):
    return pl.ds(pl.multiple_of(index * size, size), size)


def cell_lists(out_block, slot, out_blocks, slots):
    count = out_block.shape[0]
    ids = jnp.arange(count, dtype=jnp.int32)
    cell = out_block * slots + slot
    order = cell * count + ids
    place = jnp.sum((order[None, :] < order[:, None]).astype(jnp.int32), axis=1)
    members = jnp.sum(jnp.where(place[None, :] == ids[:, None], ids[None, :], 0), axis=1)
    edges = jnp.arange(out_blocks * slots + 1, dtype=jnp.int32)
    starts = jnp.sum((cell[None, :] < edges[:, None]).astype(jnp.int32), axis=1)
    return starts, members


def densify_kernel(starts, members, a_hbm, d_hbm, a_buf, d_buf, in_sem, out_sem, *, out_blocks, slots):
    count, size, _ = a_hbm.shape
    chunks = in_sem.shape[0]
    step = count // chunks

    def fetch(i):
        part = pl.ds(i * step, step)
        return pltpu.make_async_copy(a_hbm.at[part], a_buf.at[part], in_sem.at[i])

    def put(o):
        rows = block(o, size)
        return pltpu.make_async_copy(d_buf.at[rows], d_hbm.at[rows], out_sem.at[o])

    for i in range(chunks):
        fetch(i).start()
    for i in range(chunks):
        fetch(i).wait()

    def one_row(o, _):
        def one_cell(t, _):
            at = o * slots + t
            total = lax.fori_loop(
                starts[at],
                starts[at + 1],
                lambda k, s: s + a_buf[members[k]].astype(jnp.float32),
                jnp.zeros((size, size), jnp.float32),
            )
            d_buf[block(o, size), block(t, size)] = total.astype(jnp.bfloat16)
            return 0

        lax.fori_loop(0, slots, one_cell, 0)
        put(o).start()
        return 0

    lax.fori_loop(0, out_blocks, one_row, 0)
    for o in range(out_blocks):
        put(o).wait()


def densify(starts, members, edges, out_blocks, slots):
    count, size, _ = edges.shape
    shape = (out_blocks * size, slots * size)
    return pl.pallas_call(
        functools.partial(densify_kernel, out_blocks=out_blocks, slots=slots),
        out_shape=jax.ShapeDtypeStruct(shape, jnp.bfloat16),
        in_specs=[SMEM, SMEM, ANY],
        out_specs=ANY,
        scratch_shapes=[
            pltpu.VMEM(edges.shape, jnp.bfloat16),
            pltpu.VMEM(shape, jnp.bfloat16),
            pltpu.SemaphoreType.DMA((math.gcd(count, 16),)),
            pltpu.SemaphoreType.DMA((out_blocks,)),
        ],
        compiler_params=pltpu.CompilerParams(vmem_limit_bytes=40 << 20),
        cost_estimate=pl.CostEstimate(flops=0, bytes_accessed=4 * edges.size, transcendentals=0),
        name="densify",
    )(starts, members, edges)


def pick_kernel(chooser, *refs):
    pieces, (out, table, in_sem, out_sem) = refs[:-4], refs[-4:]
    each = pieces[0].shape[0]
    fetches = [
        pltpu.make_async_copy(piece, table.at[pl.ds(i * each, each)], in_sem.at[i])
        for i, piece in enumerate(pieces)
    ]
    for copy in fetches:
        copy.start()
    for copy in fetches:
        copy.wait()
    puts = [
        pltpu.make_async_copy(table.at[chooser[n]], out.at[n], out_sem.at[n])
        for n in range(out.shape[0])
    ]
    for copy in puts:
        copy.start()
    for copy in puts:
        copy.wait()


def pick_blocks(chooser, pieces):
    each, size, width = pieces[0].shape
    picks = chooser.shape[0]
    return pl.pallas_call(
        pick_kernel,
        out_shape=jax.ShapeDtypeStruct((picks, size, width), jnp.bfloat16),
        in_specs=[SMEM] + [ANY] * len(pieces),
        out_specs=ANY,
        scratch_shapes=[
            pltpu.VMEM((len(pieces) * each, size, width), jnp.bfloat16),
            pltpu.SemaphoreType.DMA((len(pieces),)),
            pltpu.SemaphoreType.DMA((picks,)),
        ],
        compiler_params=pltpu.CompilerParams(vmem_limit_bytes=8 << 20),
        cost_estimate=pl.CostEstimate(
            flops=0, bytes_accessed=4 * picks * size * width, transcendentals=0
        ),
        name="pick_blocks",
    )(chooser, *pieces)


def layer_kernel(
    d_hbm, table, weight, cotangent, activ, wgrad, slot_grad, d_buf, row_grad, sem, *, row_step, col_step
):
    rows, cols = d_hbm.shape
    steps = rows // row_step
    size = slot_grad.shape[2]
    per_step = col_step // size

    def fetch(i):
        part = block(i, row_step)
        return pltpu.make_async_copy(d_hbm.at[part], d_buf.at[part], sem.at[i])

    for i in range(steps):
        fetch(i).start()
    wgrad[...] = jnp.zeros_like(wgrad)

    def forward(i, _):
        fetch(i).wait()
        part = block(i, row_step)
        agg = jnp.dot(d_buf[part, :], table[...], preferred_element_type=jnp.float32)
        agg = agg.astype(jnp.bfloat16)
        w = weight[...]
        pre = jnp.dot(agg, w, preferred_element_type=jnp.float32)
        square = pre * pre
        tanh = jnp.tanh(GELU_SCALE * (pre + GELU_CUBE * (square * pre)))
        half = 0.5 * (1.0 + tanh)
        activ[part, :] = (pre * half).astype(jnp.bfloat16)
        slope = half + (0.5 * GELU_SCALE) * pre * (1.0 - tanh * tanh) * (
            1.0 + (3 * GELU_CUBE) * square
        )
        pre_grad = (cotangent[part, :].astype(jnp.float32) * slope).astype(jnp.bfloat16)
        wgrad[...] += lax.dot_general(
            agg, pre_grad, (((0,), (0,)), ((), ())), preferred_element_type=jnp.float32
        )
        row_grad[:, part] = lax.dot_general(
            w, pre_grad, (((1,), (1,)), ((), ())), preferred_element_type=jnp.float32
        ).astype(jnp.bfloat16)
        return 0

    lax.fori_loop(0, steps, forward, 0)

    def backward(j, _):
        grad = jnp.dot(
            row_grad[...], d_buf[:, block(j, col_step)], preferred_element_type=jnp.float32
        ).astype(jnp.bfloat16)
        for q in range(per_step):
            slot_grad[j * per_step + q] = grad[:, q * size : (q + 1) * size]
        return 0

    lax.fori_loop(0, cols // col_step, backward, 0)


def layer(dense, table, weight, cotangent, size):
    rows, cols = dense.shape
    width = weight.shape[0]
    row_step, col_step = 4 * size, 4 * size
    return pl.pallas_call(
        functools.partial(layer_kernel, row_step=row_step, col_step=col_step),
        out_shape=(
            jax.ShapeDtypeStruct(cotangent.shape, jnp.bfloat16),
            jax.ShapeDtypeStruct((width, width), jnp.float32),
            jax.ShapeDtypeStruct((cols // size, width, size), jnp.bfloat16),
        ),
        in_specs=[ANY, VMEM, VMEM, VMEM],
        out_specs=(VMEM, VMEM, VMEM),
        scratch_shapes=[
            pltpu.VMEM(dense.shape, jnp.bfloat16),
            pltpu.VMEM((width, rows), jnp.bfloat16),
            pltpu.SemaphoreType.DMA((rows // row_step,)),
        ],
        compiler_params=pltpu.CompilerParams(vmem_limit_bytes=40 << 20),
        cost_estimate=pl.CostEstimate(
            flops=4 * rows * cols * width, bytes_accessed=2 * dense.size, transcendentals=0
        ),
        name="layer",
    )(dense, table, weight, cotangent)


def group_sums_kernel(place, returned, keep, send, total):
    half = keep.shape[0]
    total[...] = jnp.zeros_like(total)

    def add(n, _):
        @pl.when(place[n] >= 0)
        def _():
            total[place[n]] += returned[n].astype(jnp.float32)

        return 0

    lax.fori_loop(0, returned.shape[0], add, 0)
    keep[...] = total[:half]
    send[...] = total[half:].astype(jnp.bfloat16)


def group_sums(place, returned, groups):
    _, width, size = returned.shape
    half = (groups // 2, width, size)
    return pl.pallas_call(
        group_sums_kernel,
        out_shape=(
            jax.ShapeDtypeStruct(half, jnp.float32),
            jax.ShapeDtypeStruct(half, jnp.bfloat16),
        ),
        in_specs=[SMEM, VMEM],
        out_specs=(VMEM, VMEM),
        scratch_shapes=[pltpu.VMEM((groups, width, size), jnp.float32)],
        compiler_params=pltpu.CompilerParams(vmem_limit_bytes=16 << 20),
        cost_estimate=pl.CostEstimate(
            flops=returned.size, bytes_accessed=4 * returned.size, transcendentals=0
        ),
        name="group_sums",
    )(place, returned)


def local(features, adjacency, requests, block_coords, weight, cotangent):
    panels, span, width = features.shape
    size = adjacency.shape[-1]
    grid_rows = lax.axis_size("row")
    grid_cols = lax.axis_size("col")
    chips = grid_rows // 2
    row = lax.axis_index("row")
    chip, core = row // 2, row % 2
    out_blocks = cotangent.shape[0] // size
    wanted = requests[0, 0]
    per_peer = wanted.shape[1]
    slots = grid_cols * per_peer

    def exchange(values, axis):
        return lax.all_to_all(values, axis, split_axis=0, concat_axis=0, tiled=True)

    def to_other_core(values):
        return lax.ppermute(values, "row", [(r, r ^ 1) for r in range(grid_rows)])

    def to_chip_ahead(values, ahead):
        return lax.ppermute(
            values, "row", [(r, (r + 2 * ahead) % grid_rows) for r in range(grid_rows)]
        )

    incoming = exchange(wanted, "col").reshape(-1)
    from_panel, from_row = incoming // grid_rows, incoming % grid_rows
    other = (from_row % 2 != core).astype(jnp.int32)
    behind = (chip - from_row // 2) % chips
    ahead = (from_row // 2 - chip) % chips
    chooser = (other * chips + behind) * panels + from_panel
    chooser = jnp.where(incoming >= 0, chooser, 0)
    place = (other * chips + ahead) * panels + from_panel
    place = jnp.where(incoming >= 0, place, -1)

    mine = [features] + [to_chip_ahead(features, d) for d in range(1, chips)]
    pieces = mine + [to_other_core(piece) for piece in mine]
    sends = pick_blocks(chooser, pieces)
    table = exchange(sends, "col").reshape(slots * size, width)

    coords = block_coords[0, 0]
    starts, members = cell_lists(coords[:, 0], coords[:, 1], out_blocks, slots)
    dense = densify(starts, members, adjacency[0, 0], out_blocks, slots)

    activations, local_wgrad, slot_grad = layer(dense, table, weight, cotangent, size)

    returned = exchange(slot_grad, "col")
    keep, send = group_sums(place, returned, panels * grid_rows)
    chip_sum = keep + to_other_core(send).astype(jnp.float32)
    chip_sum = chip_sum.reshape(chips, panels, width, size)
    owned = chip_sum[0]
    for d in range(1, chips):
        owned = owned + to_chip_ahead(chip_sum[d].astype(jnp.bfloat16), d).astype(jnp.float32)
    feature_grad = jnp.swapaxes(owned, 1, 2).astype(jnp.bfloat16)

    strip = width // grid_cols
    strips = exchange(local_wgrad, "col").reshape(grid_cols, strip, width).sum(0)
    copies = jnp.broadcast_to(strips[None], (grid_rows, strip, width))
    strips = exchange(copies, "row").sum(0)
    copies = jnp.broadcast_to(strips[None], (grid_cols, strip, width))
    weight_grad = exchange(copies, "col").reshape(width, width)
    return (activations, weight_grad, feature_grad)


def solution(mesh):
    placed = (
        P(None, ("row", "col"), None),
        P("row", "col", None, None, None),
        P("row", "col", None, None),
        P("row", "col", None, None),
        P(),
        P(("row", "col"), None),
    )
    return jax.shard_map(
        local,
        mesh=mesh,
        in_specs=placed,
        out_specs=(P(("row", "col"), None), P(), P(None, ("row", "col"), None)),
        check_vma=False,
    )
```

```python
import functools
import math

import jax
import jax.numpy as jnp
from jax import lax
from jax.experimental import pallas as pl
from jax.experimental.pallas import tpu as pltpu
from jax.sharding import PartitionSpec as P

GELU_SCALE = math.sqrt(2 / math.pi)
GELU_CUBE = 0.044715
SMEM = pl.BlockSpec(memory_space=pltpu.SMEM)
VMEM = pl.BlockSpec(memory_space=pltpu.VMEM)
ANY = pl.BlockSpec(memory_space=pl.ANY)


def block(index, size):
    return pl.ds(pl.multiple_of(index * size, size), size)


def cell_lists(out_block, slot, out_blocks, slots):
    count = out_block.shape[0]
    ids = jnp.arange(count, dtype=jnp.int32)
    cell = out_block * slots + slot
    order = cell * count + ids
    place = jnp.sum((order[None, :] < order[:, None]).astype(jnp.int32), axis=1)
    members = jnp.sum(jnp.where(place[None, :] == ids[:, None], ids[None, :], 0), axis=1)
    edges = jnp.arange(out_blocks * slots + 1, dtype=jnp.int32)
    starts = jnp.sum((cell[None, :] < edges[:, None]).astype(jnp.int32), axis=1)
    return starts, members


def densify_kernel(starts, members, a_hbm, *refs, out_blocks, slots, core):
    d_hbm, a_buf, d_buf, in_sem, out_sem = refs[-5:]
    count, size, _ = a_hbm.shape
    chunks = in_sem.shape[0]
    step = count // chunks

    def fetch(i):
        part = pl.ds(i * step, step)
        return pltpu.make_async_copy(a_hbm.at[part], a_buf.at[part], in_sem.at[i])

    def put(o):
        rows = block(o, size)
        return pltpu.make_async_copy(d_buf.at[rows], d_hbm.at[rows], out_sem.at[o])

    @pl.when(lax.axis_index("row") % 2 == core)
    def _():
        for i in range(chunks):
            fetch(i).start()
        for i in range(chunks):
            fetch(i).wait()

        def one_row(o, _):
            def one_cell(t, _):
                at = o * slots + t
                total = lax.fori_loop(
                    starts[at],
                    starts[at + 1],
                    lambda k, s: s + a_buf[members[k]].astype(jnp.float32),
                    jnp.zeros((size, size), jnp.float32),
                )
                d_buf[block(o, size), block(t, size)] = total.astype(jnp.bfloat16)
                return 0

            lax.fori_loop(0, slots, one_cell, 0)
            put(o).start()
            return 0

        lax.fori_loop(0, out_blocks, one_row, 0)
        for o in range(out_blocks):
            put(o).wait()


def densify(starts, members, edges, out_blocks, slots, core, before=()):
    count, size, _ = edges.shape
    shape = (out_blocks * size, slots * size)
    return pl.pallas_call(
        functools.partial(densify_kernel, out_blocks=out_blocks, slots=slots, core=core),
        out_shape=jax.ShapeDtypeStruct(shape, jnp.bfloat16),
        in_specs=[SMEM, SMEM, ANY] + [ANY] * len(before),
        out_specs=ANY,
        input_output_aliases={3 + i: i for i in range(len(before))},
        scratch_shapes=[
            pltpu.VMEM(edges.shape, jnp.bfloat16),
            pltpu.VMEM(shape, jnp.bfloat16),
            pltpu.SemaphoreType.DMA((math.gcd(count, 16),)),
            pltpu.SemaphoreType.DMA((out_blocks,)),
        ],
        compiler_params=pltpu.CompilerParams(vmem_limit_bytes=40 << 20),
        cost_estimate=pl.CostEstimate(flops=0, bytes_accessed=4 * edges.size, transcendentals=0),
        name="densify",
    )(starts, members, edges, *before)


def block_place(wanted, row, chips, panels, ahead):
    panel, owner = wanted // (2 * chips), wanted % (2 * chips)
    way = owner // 2 - row // 2
    distance = (way if ahead else -way) % chips
    return ((owner % 2 != row % 2).astype(jnp.int32) * chips + distance) * panels + panel


def pick_kernel(incoming, *refs):
    pieces, (out, table, in_sem, out_sem) = refs[:-4], refs[-4:]
    each = pieces[0].shape[0]
    peers, per_peer = incoming.shape
    row = lax.axis_index("row")
    fetches = [
        pltpu.make_async_copy(piece, table.at[pl.ds(i * each, each)], in_sem.at[i])
        for i, piece in enumerate(pieces)
    ]
    for copy in fetches:
        copy.start()
    for copy in fetches:
        copy.wait()
    puts = []
    for n in range(out.shape[0]):
        wanted = jnp.maximum(incoming[n // per_peer, n % per_peer], 0)
        at = block_place(wanted, row, len(pieces) // 2, each, False)
        puts.append(pltpu.make_async_copy(table.at[at], out.at[n], out_sem.at[n]))
    for copy in puts:
        copy.start()
    for copy in puts:
        copy.wait()


def pick_blocks(incoming, pieces):
    each, size, width = pieces[0].shape
    picks = incoming.size
    return pl.pallas_call(
        pick_kernel,
        out_shape=jax.ShapeDtypeStruct((picks, size, width), jnp.bfloat16),
        in_specs=[SMEM] + [ANY] * len(pieces),
        out_specs=ANY,
        scratch_shapes=[
            pltpu.VMEM((len(pieces) * each, size, width), jnp.bfloat16),
            pltpu.SemaphoreType.DMA((len(pieces),)),
            pltpu.SemaphoreType.DMA((picks,)),
        ],
        compiler_params=pltpu.CompilerParams(vmem_limit_bytes=8 << 20),
        cost_estimate=pl.CostEstimate(
            flops=0, bytes_accessed=4 * picks * size * width, transcendentals=0
        ),
        name="pick_blocks",
    )(incoming, *pieces)


def layer_kernel(
    dense, table, weight, cotangent, activ, grads,
    d_buf, act_buf, grad_buf, wgrad, row_grad, d_sem, act_sem, grad_sem,
):
    rows, cols = dense.shape
    peers, _, size = grads.shape
    width = weight.shape[0]
    steps = act_sem.shape[0]
    row_step = rows // steps
    col_step = cols // grad_sem.shape[0]
    per_peer = cols // size // peers
    peers_done = col_step // size // per_peer

    def fetch(i):
        part = block(i, row_step)
        return pltpu.make_async_copy(dense.at[part], d_buf.at[part], d_sem.at[i])

    def put_activ(i):
        part = block(i, row_step)
        return pltpu.make_async_copy(act_buf.at[part], activ.at[part], act_sem.at[i])

    def put_grads(j):
        part = pl.ds(j * peers_done, peers_done)
        return pltpu.make_async_copy(grad_buf.at[part], grads.at[part], grad_sem.at[j])

    for i in range(steps):
        fetch(i).start()
    wgrad[...] = jnp.zeros_like(wgrad)

    def forward(i, _):
        fetch(i).wait()
        part = block(i, row_step)
        agg = jnp.dot(d_buf[part, :], table[...], preferred_element_type=jnp.float32)
        agg = agg.astype(jnp.bfloat16)
        w = weight[...]
        pre = jnp.dot(agg, w, preferred_element_type=jnp.float32)
        square = pre * pre
        tanh = jnp.tanh(GELU_SCALE * (pre + GELU_CUBE * (square * pre)))
        half = 0.5 * (1.0 + tanh)
        act_buf[part, :] = (pre * half).astype(jnp.bfloat16)
        slope = half + (0.5 * GELU_SCALE) * pre * (1.0 - tanh * tanh) * (
            1.0 + (3 * GELU_CUBE) * square
        )
        pre_grad = (cotangent[part, :].astype(jnp.float32) * slope).astype(jnp.bfloat16)
        wgrad[...] += lax.dot_general(
            agg, pre_grad, (((0,), (0,)), ((), ())), preferred_element_type=jnp.float32
        )
        row_grad[:, part] = lax.dot_general(
            w, pre_grad, (((1,), (1,)), ((), ())), preferred_element_type=jnp.float32
        ).astype(jnp.bfloat16)
        put_activ(i).start()
        return 0

    lax.fori_loop(0, steps, forward, 0)

    strip = width // peers
    for p in range(peers):
        rows_of_p = wgrad[p * strip : (p + 1) * strip, :].astype(jnp.bfloat16)
        for q in range(width // size):
            at = per_peer * width + q * strip
            grad_buf[p, at : at + strip] = rows_of_p[:, q * size : (q + 1) * size]

    def backward(j, _):
        grad = jnp.dot(
            row_grad[...], d_buf[:, block(j, col_step)], preferred_element_type=jnp.float32
        ).astype(jnp.bfloat16)
        for p in range(peers_done):
            for q in range(per_peer):
                at = (p * per_peer + q) * size
                grad_buf[j * peers_done + p, q * width : (q + 1) * width] = grad[:, at : at + size]
        put_grads(j).start()
        return 0

    lax.fori_loop(0, cols // col_step, backward, 0)
    for i in range(steps):
        put_activ(i).wait()
    for j in range(cols // col_step):
        put_grads(j).wait()


def layer(dense, table, weight, cotangent, size, peers):
    rows, cols = dense.shape
    width = weight.shape[0]
    sent_rows = cols // size // peers * width + width // peers * (width // size)
    row_step, col_step = 4 * size, 4 * size
    grads = jax.ShapeDtypeStruct((peers, sent_rows, size), jnp.bfloat16)
    return pl.pallas_call(
        layer_kernel,
        out_shape=(jax.ShapeDtypeStruct(cotangent.shape, jnp.bfloat16), grads),
        in_specs=[ANY, VMEM, VMEM, VMEM],
        out_specs=(ANY, ANY),
        scratch_shapes=[
            pltpu.VMEM(dense.shape, jnp.bfloat16),
            pltpu.VMEM(cotangent.shape, jnp.bfloat16),
            pltpu.VMEM(grads.shape, jnp.bfloat16),
            pltpu.VMEM((width, width), jnp.float32),
            pltpu.VMEM((width, rows), jnp.bfloat16),
            pltpu.SemaphoreType.DMA((rows // row_step,)),
            pltpu.SemaphoreType.DMA((rows // row_step,)),
            pltpu.SemaphoreType.DMA((cols // col_step,)),
        ],
        compiler_params=pltpu.CompilerParams(vmem_limit_bytes=40 << 20),
        cost_estimate=pl.CostEstimate(
            flops=4 * rows * cols * width, bytes_accessed=2 * dense.size, transcendentals=0
        ),
        name="layer",
    )(dense, table, weight, cotangent)


def group_sums_kernel(incoming, returned, keep, send, total):
    half, width, _ = keep.shape
    peers, per_peer = incoming.shape
    row = lax.axis_index("row")
    chips = lax.axis_size("row") // 2
    total[...] = jnp.zeros_like(total)

    def add(peer, _):
        for j in range(per_peer):
            wanted = incoming[peer, j]

            @pl.when(wanted >= 0)
            def _():
                at = block_place(jnp.maximum(wanted, 0), row, chips, half // chips, True)
                total[at] += returned[peer, j * width : (j + 1) * width].astype(jnp.float32)

        return 0

    lax.fori_loop(0, peers, add, 0)
    keep[...] = total[:half]
    send[...] = total[half:].astype(jnp.bfloat16)


def group_sums(incoming, returned, groups, width):
    size = returned.shape[2]
    half = (groups // 2, width, size)
    return pl.pallas_call(
        group_sums_kernel,
        out_shape=(
            jax.ShapeDtypeStruct(half, jnp.float32),
            jax.ShapeDtypeStruct(half, jnp.bfloat16),
        ),
        in_specs=[SMEM, VMEM],
        out_specs=(VMEM, VMEM),
        scratch_shapes=[pltpu.VMEM((groups, width, size), jnp.float32)],
        compiler_params=pltpu.CompilerParams(vmem_limit_bytes=16 << 20),
        cost_estimate=pl.CostEstimate(
            flops=returned.size, bytes_accessed=4 * returned.size, transcendentals=0
        ),
        name="group_sums",
    )(incoming, returned)


def chip_sums_kernel(keep, arrived, own, *messages):
    panels = own.shape[0]
    for d in range(1 + len(messages)):
        for p in range(panels):
            total = keep[d * panels + p] + arrived[d * panels + p].astype(jnp.float32)
            if d == 0:
                own[p] = total
            else:
                messages[d - 1][p] = total.astype(jnp.bfloat16)


def chip_sums(keep, arrived, chips):
    half, width, size = keep.shape
    each = (half // chips, width, size)
    shapes = [jax.ShapeDtypeStruct(each, jnp.float32)]
    shapes += [jax.ShapeDtypeStruct(each, jnp.bfloat16)] * (chips - 1)
    return pl.pallas_call(
        chip_sums_kernel,
        out_shape=shapes,
        in_specs=[VMEM] * 2,
        out_specs=[VMEM] * chips,
        compiler_params=pltpu.CompilerParams(vmem_limit_bytes=8 << 20),
        cost_estimate=pl.CostEstimate(flops=keep.size, bytes_accessed=8 * keep.size, transcendentals=0),
        name="chip_sums",
    )(keep, arrived)


def owner_sum_kernel(own, *refs):
    parts, out = refs[:-1], refs[-1]
    for p in range(out.shape[0]):
        total = own[p]
        for part in parts:
            total = total + part[p].astype(jnp.float32)
        out[p] = total.T.astype(jnp.bfloat16)


def owner_sum(own, parts):
    panels, width, size = own.shape
    return pl.pallas_call(
        owner_sum_kernel,
        out_shape=jax.ShapeDtypeStruct((panels, size, width), jnp.bfloat16),
        in_specs=[VMEM] * (1 + len(parts)),
        out_specs=VMEM,
        compiler_params=pltpu.CompilerParams(vmem_limit_bytes=8 << 20),
        cost_estimate=pl.CostEstimate(flops=own.size, bytes_accessed=8 * own.size, transcendentals=0),
        name="owner_sum",
    )(own, *parts)


def local(features, adjacency, requests, block_coords, weight, cotangent):
    panels, span, width = features.shape
    size = adjacency.shape[-1]
    grid_rows = lax.axis_size("row")
    grid_cols = lax.axis_size("col")
    chips = grid_rows // 2
    out_blocks = cotangent.shape[0] // size
    wanted = requests[0, 0]
    per_peer = wanted.shape[1]
    slots = grid_cols * per_peer

    def exchange(values, axis):
        return lax.all_to_all(values, axis, split_axis=0, concat_axis=0, tiled=True)

    def to_other_core(values):
        return lax.ppermute(values, "row", [(r, r ^ 1) for r in range(grid_rows)])

    def to_chip_ahead(values, ahead):
        return lax.ppermute(
            values, "row", [(r, (r + 2 * ahead) % grid_rows) for r in range(grid_rows)]
        )

    incoming = exchange(wanted, "col")
    mine = [features] + [to_chip_ahead(features, d) for d in range(1, chips)]
    incoming, *mine = lax.optimization_barrier((incoming, *mine))
    pieces = mine + [to_other_core(piece) for piece in mine]
    sends = pick_blocks(incoming, pieces)

    coords = block_coords[0, 0]
    starts, members = cell_lists(coords[:, 0], coords[:, 1], out_blocks, slots)
    edges = adjacency[0, 0]
    dense = densify(starts, members, edges, out_blocks, slots, 1)
    sends, dense = lax.optimization_barrier((sends, dense))
    table = exchange(sends, "col").reshape(slots * size, width)
    dense = densify(starts, members, edges, out_blocks, slots, 0, (dense,))

    activations, grads = layer(dense, table, weight, cotangent, size, grid_cols)

    returned = exchange(grads, "col")
    strip = jnp.sum(returned[:, per_peer * width :].astype(jnp.float32), axis=0)

    strip = strip + to_other_core(strip)
    near = [strip] + [to_chip_ahead(strip, d) for d in range(1, chips)]
    strip = sum(near[2::2], near[0]) + sum(near[3::2], near[1])

    keep, send = group_sums(incoming, returned, panels * grid_rows, width)
    own, *messages = chip_sums(keep, to_other_core(send), chips)
    strip, *messages = lax.optimization_barrier((strip, *messages))
    parts = [to_chip_ahead(message, d + 1) for d, message in enumerate(messages)]
    feature_grad = owner_sum(own, parts)

    copies = jnp.broadcast_to(strip[None], (grid_cols, *strip.shape))
    strips = exchange(copies, "col").reshape(grid_cols, width // size, width // grid_cols, size)
    weight_grad = jnp.swapaxes(strips, 1, 2).reshape(width, width)
    return (activations, weight_grad, feature_grad)


def solution(mesh):
    placed = (
        P(None, ("row", "col"), None),
        P("row", "col", None, None, None),
        P("row", "col", None, None),
        P("row", "col", None, None),
        P(),
        P(("row", "col"), None),
    )
    return jax.shard_map(
        local,
        mesh=mesh,
        in_specs=placed,
        out_specs=(P(("row", "col"), None), P(), P(None, ("row", "col"), None)),
        check_vma=False,
    )
```

```python
import functools
import math

import jax
import jax.numpy as jnp
from jax import lax
from jax.experimental import pallas as pl
from jax.experimental.pallas import tpu as pltpu
from jax.sharding import PartitionSpec as P

GELU_SCALE = math.sqrt(2 / math.pi)
GELU_CUBE = 0.044715
SMEM = pl.BlockSpec(memory_space=pltpu.SMEM)
VMEM = pl.BlockSpec(memory_space=pltpu.VMEM)
ANY = pl.BlockSpec(memory_space=pl.ANY)


def block(index, size):
    return pl.ds(pl.multiple_of(index * size, size), size)


def cell_lists(out_block, slot, out_blocks, slots):
    count = out_block.shape[0]
    cells = out_blocks * slots
    ids = jnp.arange(count, dtype=jnp.int32)
    cell = out_block * slots + slot
    order = cell * count + ids
    place = jnp.sum((order[None, :] < order[:, None]).astype(jnp.int32), axis=1)
    members = jnp.sum(jnp.where(place[None, :] == ids[:, None], ids[None, :], 0), axis=1)
    edges = jnp.arange(cells + 1, dtype=jnp.int32)
    starts = jnp.sum((cell[None, :] < edges[:, None]).astype(jnp.int32), axis=1)
    earlier = (cell[None, :] == cell[:, None]) & (ids[None, :] < ids[:, None])
    target = jnp.where(jnp.any(earlier, axis=1), cells, cell)
    several = (starts[1:] - starts[:-1] > 1).astype(jnp.int32)
    ahead = jnp.sum(jnp.where(edges[None, :-1] < edges[:, None], several[None, :], 0), axis=1)
    turn = jnp.where(several > 0, ahead[:-1], -1)
    at = jnp.arange(count // 2, dtype=jnp.int32)
    shared = jnp.sum(jnp.where(turn[None, :] == at[:, None], edges[None, :-1], 0), axis=1)
    return target, members, starts, shared, ahead[:: slots]


def densify_kernel(target, members, starts, shared, ends, a_hbm, *refs, out_blocks, slots, core):
    d_hbm, a_buf, d_buf, in_sem, out_sem = refs[-5:]
    count, size, _ = a_hbm.shape
    chunks = in_sem.shape[0]
    step = count // chunks

    def fetch(i):
        part = pl.ds(i * step, step)
        return pltpu.make_async_copy(a_hbm.at[part], a_buf.at[part], in_sem.at[i])

    def put(o):
        rows = block(o, size)
        return pltpu.make_async_copy(d_buf.at[rows], d_hbm.at[rows], out_sem.at[o])

    def store(cell, values):
        d_buf[block(cell // slots, size), block(cell % slots, size)] = values

    @pl.when(lax.axis_index("row") % 2 == core)
    def _():
        for i in range(chunks):
            fetch(i).start()

        def clear(o, _):
            d_buf[block(o, size), :] = jnp.zeros((size, slots * size), jnp.bfloat16)
            return 0

        lax.fori_loop(0, out_blocks, clear, 0)

        def lay(i, _):
            fetch(i).wait()

            def eight(j, _):
                for q in range(8):
                    k = i * step + j * 8 + q
                    store(target[k], a_buf[k])
                return 0

            lax.fori_loop(0, step // 8, eight, 0)
            return 0

        lax.fori_loop(0, chunks, lay, 0)

        def one_row(o, _):
            def one_cell(j, _):
                cell = shared[j]
                first = starts[cell]
                total = a_buf[members[first]].astype(jnp.float32)
                total = total + a_buf[members[first + 1]].astype(jnp.float32)
                total = lax.fori_loop(
                    first + 2,
                    starts[cell + 1],
                    lambda k, s: s + a_buf[members[k]].astype(jnp.float32),
                    total,
                )
                store(cell, total.astype(jnp.bfloat16))
                return 0

            lax.fori_loop(ends[o], ends[o + 1], one_cell, 0)
            put(o).start()
            return 0

        lax.fori_loop(0, out_blocks, one_row, 0)
        for o in range(out_blocks):
            put(o).wait()


def densify(lists, edges, out_blocks, slots, core, before=()):
    count, size, _ = edges.shape
    shape = (out_blocks * size, slots * size)
    return pl.pallas_call(
        functools.partial(densify_kernel, out_blocks=out_blocks, slots=slots, core=core),
        out_shape=jax.ShapeDtypeStruct(shape, jnp.bfloat16),
        in_specs=[SMEM] * len(lists) + [ANY] * (1 + len(before)),
        out_specs=ANY,
        input_output_aliases={len(lists) + 1 + i: i for i in range(len(before))},
        scratch_shapes=[
            pltpu.VMEM(edges.shape, jnp.bfloat16),
            pltpu.VMEM((shape[0] + size, shape[1]), jnp.bfloat16),
            pltpu.SemaphoreType.DMA((math.gcd(count, 16),)),
            pltpu.SemaphoreType.DMA((out_blocks,)),
        ],
        compiler_params=pltpu.CompilerParams(vmem_limit_bytes=40 << 20),
        cost_estimate=pl.CostEstimate(flops=0, bytes_accessed=4 * edges.size, transcendentals=0),
        name="densify",
    )(*lists, edges, *before)


def block_place(wanted, row, chips, panels, ahead):
    panel, owner = wanted // (2 * chips), wanted % (2 * chips)
    way = owner // 2 - row // 2
    distance = (way if ahead else -way) % chips
    return ((owner % 2 != row % 2).astype(jnp.int32) * chips + distance) * panels + panel


def pick_kernel(incoming, *refs):
    pieces, (out, table, in_sem, out_sem) = refs[:-4], refs[-4:]
    each = pieces[0].shape[0]
    peers, per_peer = incoming.shape
    row = lax.axis_index("row")
    fetches = [
        pltpu.make_async_copy(piece, table.at[pl.ds(i * each, each)], in_sem.at[i])
        for i, piece in enumerate(pieces)
    ]
    for copy in fetches:
        copy.start()
    for copy in fetches:
        copy.wait()
    puts = []
    for n in range(out.shape[0]):
        wanted = jnp.maximum(incoming[n // per_peer, n % per_peer], 0)
        at = block_place(wanted, row, len(pieces) // 2, each, False)
        puts.append(pltpu.make_async_copy(table.at[at], out.at[n], out_sem.at[n]))
    for copy in puts:
        copy.start()
    for copy in puts:
        copy.wait()


def pick_blocks(incoming, pieces):
    each, size, width = pieces[0].shape
    picks = incoming.size
    return pl.pallas_call(
        pick_kernel,
        out_shape=jax.ShapeDtypeStruct((picks, size, width), jnp.bfloat16),
        in_specs=[SMEM] + [ANY] * len(pieces),
        out_specs=ANY,
        scratch_shapes=[
            pltpu.VMEM((len(pieces) * each, size, width), jnp.bfloat16),
            pltpu.SemaphoreType.DMA((len(pieces),)),
            pltpu.SemaphoreType.DMA((picks,)),
        ],
        compiler_params=pltpu.CompilerParams(vmem_limit_bytes=8 << 20),
        cost_estimate=pl.CostEstimate(
            flops=0, bytes_accessed=4 * picks * size * width, transcendentals=0
        ),
        name="pick_blocks",
    )(incoming, *pieces)


def layer_kernel(
    dense, table, weight, cotangent, activ, grads,
    d_buf, act_buf, grad_buf, wgrad, row_grad, d_sem, act_sem, grad_sem,
):
    rows, cols = dense.shape
    peers, _, size = grads.shape
    width = weight.shape[0]
    steps = act_sem.shape[0]
    row_step = rows // steps
    col_step = cols // grad_sem.shape[0]
    per_peer = cols // size // peers
    peers_done = col_step // size // per_peer

    def fetch(i):
        part = block(i, row_step)
        return pltpu.make_async_copy(dense.at[part], d_buf.at[part], d_sem.at[i])

    def put_activ(i):
        part = block(i, row_step)
        return pltpu.make_async_copy(act_buf.at[part], activ.at[part], act_sem.at[i])

    def put_grads(j):
        part = pl.ds(j * peers_done, peers_done)
        return pltpu.make_async_copy(grad_buf.at[part], grads.at[part], grad_sem.at[j])

    for i in range(steps):
        fetch(i).start()
    wgrad[...] = jnp.zeros_like(wgrad)

    def forward(i, _):
        fetch(i).wait()
        part = block(i, row_step)
        agg = jnp.dot(d_buf[part, :], table[...], preferred_element_type=jnp.float32)
        agg = agg.astype(jnp.bfloat16)
        w = weight[...]
        pre = jnp.dot(agg, w, preferred_element_type=jnp.float32)
        square = pre * pre
        tanh = jnp.tanh(GELU_SCALE * (pre + GELU_CUBE * (square * pre)))
        half = 0.5 * (1.0 + tanh)
        act_buf[part, :] = (pre * half).astype(jnp.bfloat16)
        slope = half + (0.5 * GELU_SCALE) * pre * (1.0 - tanh * tanh) * (
            1.0 + (3 * GELU_CUBE) * square
        )
        pre_grad = (cotangent[part, :].astype(jnp.float32) * slope).astype(jnp.bfloat16)
        wgrad[...] += lax.dot_general(
            agg, pre_grad, (((0,), (0,)), ((), ())), preferred_element_type=jnp.float32
        )
        row_grad[:, part] = lax.dot_general(
            w, pre_grad, (((1,), (1,)), ((), ())), preferred_element_type=jnp.float32
        ).astype(jnp.bfloat16)
        put_activ(i).start()
        return 0

    lax.fori_loop(0, steps, forward, 0)

    strip = width // peers
    for p in range(peers):
        rows_of_p = wgrad[p * strip : (p + 1) * strip, :].astype(jnp.bfloat16)
        for q in range(width // size):
            at = per_peer * width + q * strip
            grad_buf[p, at : at + strip] = rows_of_p[:, q * size : (q + 1) * size]

    def backward(j, _):
        grad = jnp.dot(
            row_grad[...], d_buf[:, block(j, col_step)], preferred_element_type=jnp.float32
        ).astype(jnp.bfloat16)
        for p in range(peers_done):
            for q in range(per_peer):
                at = (p * per_peer + q) * size
                grad_buf[j * peers_done + p, q * width : (q + 1) * width] = grad[:, at : at + size]
        put_grads(j).start()
        return 0

    lax.fori_loop(0, cols // col_step, backward, 0)
    for i in range(steps):
        put_activ(i).wait()
    for j in range(cols // col_step):
        put_grads(j).wait()


def layer(dense, table, weight, cotangent, size, peers):
    rows, cols = dense.shape
    width = weight.shape[0]
    sent_rows = cols // size // peers * width + width // peers * (width // size)
    row_step, col_step = 4 * size, 8 * size
    grads = jax.ShapeDtypeStruct((peers, sent_rows, size), jnp.bfloat16)
    return pl.pallas_call(
        layer_kernel,
        out_shape=(jax.ShapeDtypeStruct(cotangent.shape, jnp.bfloat16), grads),
        in_specs=[ANY, VMEM, VMEM, VMEM],
        out_specs=(ANY, ANY),
        scratch_shapes=[
            pltpu.VMEM(dense.shape, jnp.bfloat16),
            pltpu.VMEM(cotangent.shape, jnp.bfloat16),
            pltpu.VMEM(grads.shape, jnp.bfloat16),
            pltpu.VMEM((width, width), jnp.float32),
            pltpu.VMEM((width, rows), jnp.bfloat16),
            pltpu.SemaphoreType.DMA((rows // row_step,)),
            pltpu.SemaphoreType.DMA((rows // row_step,)),
            pltpu.SemaphoreType.DMA((cols // col_step,)),
        ],
        compiler_params=pltpu.CompilerParams(vmem_limit_bytes=40 << 20),
        cost_estimate=pl.CostEstimate(
            flops=4 * rows * cols * width, bytes_accessed=2 * dense.size, transcendentals=0
        ),
        name="layer",
    )(dense, table, weight, cotangent)


def group_sums_kernel(incoming, returned, keep, send, total):
    half, width, _ = keep.shape
    peers, per_peer = incoming.shape
    row = lax.axis_index("row")
    chips = lax.axis_size("row") // 2
    total[...] = jnp.zeros_like(total)

    def add(peer, _):
        for j in range(per_peer):
            wanted = incoming[peer, j]

            @pl.when(wanted >= 0)
            def _():
                at = block_place(jnp.maximum(wanted, 0), row, chips, half // chips, True)
                total[at] += returned[peer, j * width : (j + 1) * width].astype(jnp.float32)

        return 0

    lax.fori_loop(0, peers, add, 0)
    keep[...] = total[:half]
    send[...] = total[half:].astype(jnp.bfloat16)


def group_sums(incoming, returned, groups, width):
    size = returned.shape[2]
    half = (groups // 2, width, size)
    return pl.pallas_call(
        group_sums_kernel,
        out_shape=(
            jax.ShapeDtypeStruct(half, jnp.float32),
            jax.ShapeDtypeStruct(half, jnp.bfloat16),
        ),
        in_specs=[SMEM, VMEM],
        out_specs=(VMEM, VMEM),
        scratch_shapes=[pltpu.VMEM((groups, width, size), jnp.float32)],
        compiler_params=pltpu.CompilerParams(vmem_limit_bytes=16 << 20),
        cost_estimate=pl.CostEstimate(
            flops=returned.size, bytes_accessed=4 * returned.size, transcendentals=0
        ),
        name="group_sums",
    )(incoming, returned)


def chip_sums_kernel(keep, arrived, own, *messages):
    panels = own.shape[0]
    for d in range(1 + len(messages)):
        for p in range(panels):
            total = keep[d * panels + p] + arrived[d * panels + p].astype(jnp.float32)
            if d == 0:
                own[p] = total
            else:
                messages[d - 1][p] = total.astype(jnp.bfloat16)


def chip_sums(keep, arrived, chips):
    half, width, size = keep.shape
    each = (half // chips, width, size)
    shapes = [jax.ShapeDtypeStruct(each, jnp.float32)]
    shapes += [jax.ShapeDtypeStruct(each, jnp.bfloat16)] * (chips - 1)
    return pl.pallas_call(
        chip_sums_kernel,
        out_shape=shapes,
        in_specs=[VMEM] * 2,
        out_specs=[VMEM] * chips,
        compiler_params=pltpu.CompilerParams(vmem_limit_bytes=8 << 20),
        cost_estimate=pl.CostEstimate(flops=keep.size, bytes_accessed=8 * keep.size, transcendentals=0),
        name="chip_sums",
    )(keep, arrived)


def owner_sum_kernel(own, *refs):
    parts, out = refs[:-1], refs[-1]
    for p in range(out.shape[0]):
        total = own[p]
        for part in parts:
            total = total + part[p].astype(jnp.float32)
        out[p] = total.T.astype(jnp.bfloat16)


def owner_sum(own, parts):
    panels, width, size = own.shape
    return pl.pallas_call(
        owner_sum_kernel,
        out_shape=jax.ShapeDtypeStruct((panels, size, width), jnp.bfloat16),
        in_specs=[VMEM] * (1 + len(parts)),
        out_specs=VMEM,
        compiler_params=pltpu.CompilerParams(vmem_limit_bytes=8 << 20),
        cost_estimate=pl.CostEstimate(flops=own.size, bytes_accessed=8 * own.size, transcendentals=0),
        name="owner_sum",
    )(own, *parts)


def local(features, adjacency, requests, block_coords, weight, cotangent):
    panels, span, width = features.shape
    size = adjacency.shape[-1]
    grid_rows = lax.axis_size("row")
    grid_cols = lax.axis_size("col")
    chips = grid_rows // 2
    out_blocks = cotangent.shape[0] // size
    wanted = requests[0, 0]
    per_peer = wanted.shape[1]
    slots = grid_cols * per_peer

    def exchange(values, axis):
        return lax.all_to_all(values, axis, split_axis=0, concat_axis=0, tiled=True)

    def to_other_core(values):
        return lax.ppermute(values, "row", [(r, r ^ 1) for r in range(grid_rows)])

    def to_chip_ahead(values, ahead):
        return lax.ppermute(
            values, "row", [(r, (r + 2 * ahead) % grid_rows) for r in range(grid_rows)]
        )

    incoming = exchange(wanted, "col")
    mine = [features] + [to_chip_ahead(features, d) for d in range(1, chips)]
    incoming, mine[2] = lax.optimization_barrier((incoming, mine[2]))
    pieces = mine + [to_other_core(piece) for piece in mine]
    sends = pick_blocks(incoming, pieces)

    coords = block_coords[0, 0]
    lists = cell_lists(coords[:, 0], coords[:, 1], out_blocks, slots)
    edges = adjacency[0, 0]
    dense = densify(lists, edges, out_blocks, slots, 1)
    sends, dense = lax.optimization_barrier((sends, dense))
    table = exchange(sends, "col").reshape(slots * size, width)
    dense = densify(lists, edges, out_blocks, slots, 0, (dense,))

    activations, grads = layer(dense, table, weight, cotangent, size, grid_cols)

    returned = exchange(grads, "col")
    strip = jnp.sum(returned[:, per_peer * width :].astype(jnp.float32), axis=0)

    strip = strip + to_other_core(strip)
    near = [strip] + [to_chip_ahead(strip, d) for d in range(1, chips)]
    strip = sum(near[2::2], near[0]) + sum(near[3::2], near[1])

    keep, send = group_sums(incoming, returned, panels * grid_rows, width)
    own, *messages = chip_sums(keep, to_other_core(send), chips)
    strip, *messages = lax.optimization_barrier((strip, *messages))
    parts = [to_chip_ahead(message, d + 1) for d, message in enumerate(messages)]

    copies = jnp.broadcast_to(strip.astype(jnp.bfloat16)[None], (grid_cols, *strip.shape))
    strips = exchange(copies, "col").reshape(grid_cols, width // size, width // grid_cols, size)
    weight_grad = jnp.swapaxes(strips, 1, 2).reshape(width, width).astype(jnp.float32)
    own, weight_grad = lax.optimization_barrier((own, weight_grad))
    feature_grad = owner_sum(own, parts)
    return (activations, weight_grad, feature_grad)


def solution(mesh):
    placed = (
        P(None, ("row", "col"), None),
        P("row", "col", None, None, None),
        P("row", "col", None, None),
        P("row", "col", None, None),
        P(),
        P(("row", "col"), None),
    )
    return jax.shard_map(
        local,
        mesh=mesh,
        in_specs=placed,
        out_specs=(P(("row", "col"), None), P(), P(None, ("row", "col"), None)),
        check_vma=False,
    )
```

```python
import functools
import math

import jax
import jax.numpy as jnp
from jax import lax
from jax.experimental import pallas as pl
from jax.experimental.pallas import tpu as pltpu
from jax.sharding import PartitionSpec as P

GELU_SCALE = math.sqrt(2 / math.pi)
GELU_CUBE = 0.044715
SMEM = pl.BlockSpec(memory_space=pltpu.SMEM)
VMEM = pl.BlockSpec(memory_space=pltpu.VMEM)
ANY = pl.BlockSpec(memory_space=pl.ANY)


def block(index, size):
    return pl.ds(pl.multiple_of(index * size, size), size)


def cell_lists(out_block, slot, out_blocks, slots):
    count = out_block.shape[0]
    cells = out_blocks * slots
    ids = jnp.arange(count, dtype=jnp.int32)
    cell = out_block * slots + slot
    order = cell * count + ids
    place = jnp.sum((order[None, :] < order[:, None]).astype(jnp.int32), axis=1)
    members = jnp.sum(jnp.where(place[None, :] == ids[:, None], ids[None, :], 0), axis=1)
    edges = jnp.arange(cells + 1, dtype=jnp.int32)
    starts = jnp.sum((cell[None, :] < edges[:, None]).astype(jnp.int32), axis=1)
    earlier = (cell[None, :] == cell[:, None]) & (ids[None, :] < ids[:, None])
    target = jnp.where(jnp.any(earlier, axis=1), cells, cell)
    several = (starts[1:] - starts[:-1] > 1).astype(jnp.int32)
    ahead = jnp.sum(jnp.where(edges[None, :-1] < edges[:, None], several[None, :], 0), axis=1)
    turn = jnp.where(several > 0, ahead[:-1], -1)
    at = jnp.arange(count // 2, dtype=jnp.int32)
    shared = jnp.sum(jnp.where(turn[None, :] == at[:, None], edges[None, :-1], 0), axis=1)
    return target, members, starts, shared, ahead[:: slots]


def densify_kernel(target, members, starts, shared, ends, a_hbm, *refs, out_blocks, slots, core):
    d_hbm, a_buf, d_buf, in_sem, out_sem = refs[-5:]
    count, size, _ = a_hbm.shape
    chunks = in_sem.shape[0]
    step = count // chunks

    def fetch(i):
        part = pl.ds(i * step, step)
        return pltpu.make_async_copy(a_hbm.at[part], a_buf.at[part], in_sem.at[i])

    def put(o):
        rows = block(o, size)
        return pltpu.make_async_copy(d_buf.at[rows], d_hbm.at[rows], out_sem.at[o])

    def store(cell, values):
        d_buf[block(cell // slots, size), block(cell % slots, size)] = values

    @pl.when(lax.axis_index("row") % 2 == core)
    def _():
        for i in range(chunks):
            fetch(i).start()

        def clear(o, _):
            d_buf[block(o, size), :] = jnp.zeros((size, slots * size), jnp.bfloat16)
            return 0

        lax.fori_loop(0, out_blocks, clear, 0)

        def lay(i, _):
            fetch(i).wait()

            def eight(j, _):
                for q in range(8):
                    k = i * step + j * 8 + q
                    store(target[k], a_buf[k])
                return 0

            lax.fori_loop(0, step // 8, eight, 0)
            return 0

        lax.fori_loop(0, chunks, lay, 0)

        def one_row(o, _):
            def one_cell(j, _):
                cell = shared[j]
                first = starts[cell]
                total = a_buf[members[first]].astype(jnp.float32)
                total = total + a_buf[members[first + 1]].astype(jnp.float32)
                total = lax.fori_loop(
                    first + 2,
                    starts[cell + 1],
                    lambda k, s: s + a_buf[members[k]].astype(jnp.float32),
                    total,
                )
                store(cell, total.astype(jnp.bfloat16))
                return 0

            lax.fori_loop(ends[o], ends[o + 1], one_cell, 0)
            put(o).start()
            return 0

        lax.fori_loop(0, out_blocks, one_row, 0)
        for o in range(out_blocks):
            put(o).wait()


def densify(lists, edges, out_blocks, slots, core, before=()):
    count, size, _ = edges.shape
    shape = (out_blocks * size, slots * size)
    return pl.pallas_call(
        functools.partial(densify_kernel, out_blocks=out_blocks, slots=slots, core=core),
        out_shape=jax.ShapeDtypeStruct(shape, jnp.bfloat16),
        in_specs=[SMEM] * len(lists) + [ANY] * (1 + len(before)),
        out_specs=ANY,
        input_output_aliases={len(lists) + 1 + i: i for i in range(len(before))},
        scratch_shapes=[
            pltpu.VMEM(edges.shape, jnp.bfloat16),
            pltpu.VMEM((shape[0] + size, shape[1]), jnp.bfloat16),
            pltpu.SemaphoreType.DMA((math.gcd(count, 16),)),
            pltpu.SemaphoreType.DMA((out_blocks,)),
        ],
        compiler_params=pltpu.CompilerParams(vmem_limit_bytes=40 << 20),
        cost_estimate=pl.CostEstimate(flops=0, bytes_accessed=4 * edges.size, transcendentals=0),
        name="densify",
    )(*lists, edges, *before)


def block_place(wanted, row, chips, panels, ahead):
    panel, owner = wanted // (2 * chips), wanted % (2 * chips)
    way = owner // 2 - row // 2
    distance = (way if ahead else -way) % chips
    return ((owner % 2 != row % 2).astype(jnp.int32) * chips + distance) * panels + panel


def pick_kernel(incoming, *refs):
    pieces, (out, table, in_sem, out_sem) = refs[:-4], refs[-4:]
    each = pieces[0].shape[0]
    peers, per_peer = incoming.shape
    row = lax.axis_index("row")
    fetches = [
        pltpu.make_async_copy(piece, table.at[pl.ds(i * each, each)], in_sem.at[i])
        for i, piece in enumerate(pieces)
    ]
    for copy in fetches:
        copy.start()
    for copy in fetches:
        copy.wait()
    puts = []
    for n in range(out.shape[0]):
        wanted = jnp.maximum(incoming[n // per_peer, n % per_peer], 0)
        at = block_place(wanted, row, len(pieces) // 2, each, False)
        puts.append(pltpu.make_async_copy(table.at[at], out.at[n], out_sem.at[n]))
    for copy in puts:
        copy.start()
    for copy in puts:
        copy.wait()


def pick_blocks(incoming, pieces):
    each, size, width = pieces[0].shape
    picks = incoming.size
    return pl.pallas_call(
        pick_kernel,
        out_shape=jax.ShapeDtypeStruct((picks, size, width), jnp.bfloat16),
        in_specs=[SMEM] + [ANY] * len(pieces),
        out_specs=ANY,
        scratch_shapes=[
            pltpu.VMEM((len(pieces) * each, size, width), jnp.bfloat16),
            pltpu.SemaphoreType.DMA((len(pieces),)),
            pltpu.SemaphoreType.DMA((picks,)),
        ],
        compiler_params=pltpu.CompilerParams(vmem_limit_bytes=8 << 20),
        cost_estimate=pl.CostEstimate(
            flops=0, bytes_accessed=4 * picks * size * width, transcendentals=0
        ),
        name="pick_blocks",
    )(incoming, *pieces)


def layer_kernel(
    dense, table, weight, cotangent, activ, grads,
    d_buf, act_buf, grad_buf, wgrad, row_grad, d_sem, act_sem, grad_sem,
):
    rows, cols = dense.shape
    peers, _, size = grads.shape
    width = weight.shape[0]
    steps = act_sem.shape[0]
    row_step = rows // steps
    col_step = cols // grad_sem.shape[0]
    per_peer = cols // size // peers
    peers_done = col_step // size // per_peer

    def fetch(i):
        part = block(i, row_step)
        return pltpu.make_async_copy(dense.at[part], d_buf.at[part], d_sem.at[i])

    def put_activ(i):
        part = block(i, row_step)
        return pltpu.make_async_copy(act_buf.at[part], activ.at[part], act_sem.at[i])

    def put_grads(j):
        part = pl.ds(j * peers_done, peers_done)
        return pltpu.make_async_copy(grad_buf.at[part], grads.at[part], grad_sem.at[j])

    for i in range(steps):
        fetch(i).start()
    wgrad[...] = jnp.zeros_like(wgrad)

    def forward(i, _):
        fetch(i).wait()
        part = block(i, row_step)
        agg = jnp.dot(d_buf[part, :], table[...], preferred_element_type=jnp.float32)
        agg = agg.astype(jnp.bfloat16)
        w = weight[...]
        pre = jnp.dot(agg, w, preferred_element_type=jnp.float32)
        square = pre * pre
        tanh = jnp.tanh(GELU_SCALE * (pre + GELU_CUBE * (square * pre)))
        half = 0.5 * (1.0 + tanh)
        act_buf[part, :] = (pre * half).astype(jnp.bfloat16)
        slope = half + (0.5 * GELU_SCALE) * pre * (1.0 - tanh * tanh) * (
            1.0 + (3 * GELU_CUBE) * square
        )
        pre_grad = (cotangent[part, :].astype(jnp.float32) * slope).astype(jnp.bfloat16)
        wgrad[...] += lax.dot_general(
            agg, pre_grad, (((0,), (0,)), ((), ())), preferred_element_type=jnp.float32
        )
        row_grad[:, part] = lax.dot_general(
            w, pre_grad, (((1,), (1,)), ((), ())), preferred_element_type=jnp.float32
        ).astype(jnp.bfloat16)
        put_activ(i).start()
        return 0

    lax.fori_loop(0, steps, forward, 0)

    strip = width // peers
    for p in range(peers):
        rows_of_p = wgrad[p * strip : (p + 1) * strip, :].astype(jnp.bfloat16)
        for q in range(width // size):
            at = per_peer * width + q * strip
            grad_buf[p, at : at + strip] = rows_of_p[:, q * size : (q + 1) * size]

    def backward(j, _):
        grad = jnp.dot(
            row_grad[...], d_buf[:, block(j, col_step)], preferred_element_type=jnp.float32
        ).astype(jnp.bfloat16)
        for p in range(peers_done):
            for q in range(per_peer):
                at = (p * per_peer + q) * size
                grad_buf[j * peers_done + p, q * width : (q + 1) * width] = grad[:, at : at + size]
        put_grads(j).start()
        return 0

    lax.fori_loop(0, cols // col_step, backward, 0)
    for i in range(steps):
        put_activ(i).wait()
    for j in range(cols // col_step):
        put_grads(j).wait()


def layer(dense, table, weight, cotangent, size, peers):
    rows, cols = dense.shape
    width = weight.shape[0]
    sent_rows = cols // size // peers * width + width // peers * (width // size)
    row_step, col_step = 4 * size, 16 * size
    grads = jax.ShapeDtypeStruct((peers, sent_rows, size), jnp.bfloat16)
    return pl.pallas_call(
        layer_kernel,
        out_shape=(jax.ShapeDtypeStruct(cotangent.shape, jnp.bfloat16), grads),
        in_specs=[ANY, VMEM, VMEM, VMEM],
        out_specs=(ANY, ANY),
        scratch_shapes=[
            pltpu.VMEM(dense.shape, jnp.bfloat16),
            pltpu.VMEM(cotangent.shape, jnp.bfloat16),
            pltpu.VMEM(grads.shape, jnp.bfloat16),
            pltpu.VMEM((width, width), jnp.float32),
            pltpu.VMEM((width, rows), jnp.bfloat16),
            pltpu.SemaphoreType.DMA((rows // row_step,)),
            pltpu.SemaphoreType.DMA((rows // row_step,)),
            pltpu.SemaphoreType.DMA((cols // col_step,)),
        ],
        compiler_params=pltpu.CompilerParams(vmem_limit_bytes=40 << 20),
        cost_estimate=pl.CostEstimate(
            flops=4 * rows * cols * width, bytes_accessed=2 * dense.size, transcendentals=0
        ),
        name="layer",
    )(dense, table, weight, cotangent)


def group_sums_kernel(incoming, returned, keep, send, total):
    half, width, _ = keep.shape
    peers, per_peer = incoming.shape
    row = lax.axis_index("row")
    chips = lax.axis_size("row") // 2
    total[...] = jnp.zeros_like(total)

    def add(peer, _):
        for j in range(per_peer):
            wanted = incoming[peer, j]

            @pl.when(wanted >= 0)
            def _():
                at = block_place(jnp.maximum(wanted, 0), row, chips, half // chips, True)
                total[at] += returned[peer, j * width : (j + 1) * width].astype(jnp.float32)

        return 0

    lax.fori_loop(0, peers, add, 0)
    keep[...] = total[:half]
    send[...] = total[half:].astype(jnp.bfloat16)


def group_sums(incoming, returned, groups, width):
    size = returned.shape[2]
    half = (groups // 2, width, size)
    return pl.pallas_call(
        group_sums_kernel,
        out_shape=(
            jax.ShapeDtypeStruct(half, jnp.float32),
            jax.ShapeDtypeStruct(half, jnp.bfloat16),
        ),
        in_specs=[SMEM, VMEM],
        out_specs=(VMEM, VMEM),
        scratch_shapes=[pltpu.VMEM((groups, width, size), jnp.float32)],
        compiler_params=pltpu.CompilerParams(vmem_limit_bytes=16 << 20),
        cost_estimate=pl.CostEstimate(
            flops=returned.size, bytes_accessed=4 * returned.size, transcendentals=0
        ),
        name="group_sums",
    )(incoming, returned)


def chip_sums_kernel(keep, arrived, own, *messages):
    panels = own.shape[0]
    for d in range(1 + len(messages)):
        for p in range(panels):
            total = keep[d * panels + p] + arrived[d * panels + p].astype(jnp.float32)
            if d == 0:
                own[p] = total
            else:
                messages[d - 1][p] = total.astype(jnp.bfloat16)


def chip_sums(keep, arrived, chips):
    half, width, size = keep.shape
    each = (half // chips, width, size)
    shapes = [jax.ShapeDtypeStruct(each, jnp.float32)]
    shapes += [jax.ShapeDtypeStruct(each, jnp.bfloat16)] * (chips - 1)
    return pl.pallas_call(
        chip_sums_kernel,
        out_shape=shapes,
        in_specs=[VMEM] * 2,
        out_specs=[VMEM] * chips,
        compiler_params=pltpu.CompilerParams(vmem_limit_bytes=8 << 20),
        cost_estimate=pl.CostEstimate(flops=keep.size, bytes_accessed=8 * keep.size, transcendentals=0),
        name="chip_sums",
    )(keep, arrived)


def owner_sum_kernel(own, *refs):
    parts, out = refs[:-1], refs[-1]
    for p in range(out.shape[0]):
        total = own[p]
        for part in parts:
            total = total + part[p].astype(jnp.float32)
        out[p] = total.T.astype(jnp.bfloat16)


def owner_sum(own, parts):
    panels, width, size = own.shape
    return pl.pallas_call(
        owner_sum_kernel,
        out_shape=jax.ShapeDtypeStruct((panels, size, width), jnp.bfloat16),
        in_specs=[VMEM] * (1 + len(parts)),
        out_specs=VMEM,
        compiler_params=pltpu.CompilerParams(vmem_limit_bytes=8 << 20),
        cost_estimate=pl.CostEstimate(flops=own.size, bytes_accessed=8 * own.size, transcendentals=0),
        name="owner_sum",
    )(own, *parts)


def local(features, adjacency, requests, block_coords, weight, cotangent):
    panels, span, width = features.shape
    size = adjacency.shape[-1]
    grid_rows = lax.axis_size("row")
    grid_cols = lax.axis_size("col")
    chips = grid_rows // 2
    out_blocks = cotangent.shape[0] // size
    wanted = requests[0, 0]
    per_peer = wanted.shape[1]
    slots = grid_cols * per_peer

    def exchange(values, axis):
        return lax.all_to_all(values, axis, split_axis=0, concat_axis=0, tiled=True)

    def to_other_core(values):
        return lax.ppermute(values, "row", [(r, r ^ 1) for r in range(grid_rows)])

    def to_chip_ahead(values, ahead):
        return lax.ppermute(
            values, "row", [(r, (r + 2 * ahead) % grid_rows) for r in range(grid_rows)]
        )

    incoming = exchange(wanted, "col")
    mine = [features] + [to_chip_ahead(features, d) for d in range(1, chips)]
    incoming, mine[2] = lax.optimization_barrier((incoming, mine[2]))
    pieces = mine + [to_other_core(piece) for piece in mine]
    sends = pick_blocks(incoming, pieces)

    coords = block_coords[0, 0]
    lists = cell_lists(coords[:, 0], coords[:, 1], out_blocks, slots)
    edges = adjacency[0, 0]
    dense = densify(lists, edges, out_blocks, slots, 1)
    sends, dense = lax.optimization_barrier((sends, dense))
    table = exchange(sends, "col").reshape(slots * size, width)
    dense = densify(lists, edges, out_blocks, slots, 0, (dense,))

    activations, grads = layer(dense, table, weight, cotangent, size, grid_cols)

    returned = exchange(grads, "col")
    strip = jnp.sum(returned[:, per_peer * width :].astype(jnp.float32), axis=0)

    strip = strip + to_other_core(strip)
    near = [strip] + [to_chip_ahead(strip, d) for d in range(1, chips)]
    strip = sum(near[2::2], near[0]) + sum(near[3::2], near[1])

    keep, send = group_sums(incoming, returned, panels * grid_rows, width)
    own, *messages = chip_sums(keep, to_other_core(send), chips)
    strip, *messages = lax.optimization_barrier((strip, *messages))
    parts = [to_chip_ahead(message, d + 1) for d, message in enumerate(messages)]

    copies = jnp.broadcast_to(strip.astype(jnp.bfloat16)[None], (grid_cols, *strip.shape))
    strips = exchange(copies, "col").reshape(grid_cols, width // size, width // grid_cols, size)
    weight_grad = jnp.swapaxes(strips, 1, 2).reshape(width, width).astype(jnp.float32)
    own, weight_grad = lax.optimization_barrier((own, weight_grad))
    feature_grad = owner_sum(own, parts)
    return (activations, weight_grad, feature_grad)


def solution(mesh):
    placed = (
        P(None, ("row", "col"), None),
        P("row", "col", None, None, None),
        P("row", "col", None, None),
        P("row", "col", None, None),
        P(),
        P(("row", "col"), None),
    )
    return jax.shard_map(
        local,
        mesh=mesh,
        in_specs=placed,
        out_specs=(P(("row", "col"), None), P(), P(None, ("row", "col"), None)),
        check_vma=False,
    )
```

```python
import functools
import math

import jax
import jax.numpy as jnp
from jax import lax
from jax.experimental import pallas as pl
from jax.experimental.pallas import tpu as pltpu
from jax.sharding import PartitionSpec as P

GELU_SCALE = math.sqrt(2 / math.pi)
GELU_CUBE = 0.044715
SMEM = pl.BlockSpec(memory_space=pltpu.SMEM)
VMEM = pl.BlockSpec(memory_space=pltpu.VMEM)
ANY = pl.BlockSpec(memory_space=pl.ANY)


def block(index, size):
    return pl.ds(pl.multiple_of(index * size, size), size)


def cell_lists(out_block, slot, out_blocks, slots):
    count = out_block.shape[0]
    cells = out_blocks * slots
    ids = jnp.arange(count, dtype=jnp.int32)
    cell = out_block * slots + slot
    order = cell * count + ids
    place = jnp.sum((order[None, :] < order[:, None]).astype(jnp.int32), axis=1)
    members = jnp.sum(jnp.where(place[None, :] == ids[:, None], ids[None, :], 0), axis=1)
    edges = jnp.arange(cells + 1, dtype=jnp.int32)
    starts = jnp.sum((cell[None, :] < edges[:, None]).astype(jnp.int32), axis=1)
    earlier = (cell[None, :] == cell[:, None]) & (ids[None, :] < ids[:, None])
    target = jnp.where(jnp.any(earlier, axis=1), cells, cell)
    several = (starts[1:] - starts[:-1] > 1).astype(jnp.int32)
    ahead = jnp.sum(jnp.where(edges[None, :-1] < edges[:, None], several[None, :], 0), axis=1)
    turn = jnp.where(several > 0, ahead[:-1], -1)
    at = jnp.arange(count // 2, dtype=jnp.int32)
    shared = jnp.sum(jnp.where(turn[None, :] == at[:, None], edges[None, :-1], 0), axis=1)
    return target, members, starts, shared, ahead[:: slots]


def densify_kernel(target, members, starts, shared, ends, a_hbm, *refs, out_blocks, slots, core):
    d_hbm, a_buf, d_buf, in_sem, out_sem = refs[-5:]
    count, size, _ = a_hbm.shape
    chunks = in_sem.shape[0]
    step = count // chunks

    def fetch(i):
        part = pl.ds(i * step, step)
        return pltpu.make_async_copy(a_hbm.at[part], a_buf.at[part], in_sem.at[i])

    def put(o):
        rows = block(o, size)
        return pltpu.make_async_copy(d_buf.at[rows], d_hbm.at[rows], out_sem.at[o])

    def store(cell, values):
        d_buf[block(cell // slots, size), block(cell % slots, size)] = values

    @pl.when(lax.axis_index("row") % 2 == core)
    def _():
        for i in range(chunks):
            fetch(i).start()

        def clear(o, _):
            d_buf[block(o, size), :] = jnp.zeros((size, slots * size), jnp.bfloat16)
            return 0

        lax.fori_loop(0, out_blocks, clear, 0)

        def lay(i, _):
            fetch(i).wait()

            def eight(j, _):
                for q in range(8):
                    k = i * step + j * 8 + q
                    store(target[k], a_buf[k])
                return 0

            lax.fori_loop(0, step // 8, eight, 0)
            return 0

        lax.fori_loop(0, chunks, lay, 0)

        def one_row(o, _):
            def one_cell(j, _):
                cell = shared[j]
                first = starts[cell]
                total = a_buf[members[first]].astype(jnp.float32)
                total = total + a_buf[members[first + 1]].astype(jnp.float32)
                total = lax.fori_loop(
                    first + 2,
                    starts[cell + 1],
                    lambda k, s: s + a_buf[members[k]].astype(jnp.float32),
                    total,
                )
                store(cell, total.astype(jnp.bfloat16))
                return 0

            lax.fori_loop(ends[o], ends[o + 1], one_cell, 0)
            put(o).start()
            return 0

        lax.fori_loop(0, out_blocks, one_row, 0)
        for o in range(out_blocks):
            put(o).wait()


def densify(lists, edges, out_blocks, slots, core, before=()):
    count, size, _ = edges.shape
    shape = (out_blocks * size, slots * size)
    return pl.pallas_call(
        functools.partial(densify_kernel, out_blocks=out_blocks, slots=slots, core=core),
        out_shape=jax.ShapeDtypeStruct(shape, jnp.bfloat16),
        in_specs=[SMEM] * len(lists) + [ANY] * (1 + len(before)),
        out_specs=ANY,
        input_output_aliases={len(lists) + 1 + i: i for i in range(len(before))},
        scratch_shapes=[
            pltpu.VMEM(edges.shape, jnp.bfloat16),
            pltpu.VMEM((shape[0] + size, shape[1]), jnp.bfloat16),
            pltpu.SemaphoreType.DMA((math.gcd(count, 16),)),
            pltpu.SemaphoreType.DMA((out_blocks,)),
        ],
        compiler_params=pltpu.CompilerParams(vmem_limit_bytes=40 << 20),
        cost_estimate=pl.CostEstimate(flops=0, bytes_accessed=4 * edges.size, transcendentals=0),
        name="densify",
    )(*lists, edges, *before)


def block_place(wanted, row, chips, panels, ahead):
    panel, owner = wanted // (2 * chips), wanted % (2 * chips)
    way = owner // 2 - row // 2
    distance = (way if ahead else -way) % chips
    return ((owner % 2 != row % 2).astype(jnp.int32) * chips + distance) * panels + panel


def pick_kernel(incoming, *refs):
    pieces, (out, table, in_sem, out_sem) = refs[:-4], refs[-4:]
    each = pieces[0].shape[0]
    peers, per_peer = incoming.shape
    row = lax.axis_index("row")
    fetches = [
        pltpu.make_async_copy(piece, table.at[pl.ds(i * each, each)], in_sem.at[i])
        for i, piece in enumerate(pieces)
    ]
    for copy in fetches:
        copy.start()
    for copy in fetches:
        copy.wait()
    puts = []
    for n in range(out.shape[0]):
        wanted = jnp.maximum(incoming[n // per_peer, n % per_peer], 0)
        at = block_place(wanted, row, len(pieces) // 2, each, False)
        puts.append(pltpu.make_async_copy(table.at[at], out.at[n], out_sem.at[n]))
    for copy in puts:
        copy.start()
    for copy in puts:
        copy.wait()


def pick_blocks(incoming, pieces):
    each, size, width = pieces[0].shape
    picks = incoming.size
    return pl.pallas_call(
        pick_kernel,
        out_shape=jax.ShapeDtypeStruct((picks, size, width), jnp.bfloat16),
        in_specs=[SMEM] + [ANY] * len(pieces),
        out_specs=ANY,
        scratch_shapes=[
            pltpu.VMEM((len(pieces) * each, size, width), jnp.bfloat16),
            pltpu.SemaphoreType.DMA((len(pieces),)),
            pltpu.SemaphoreType.DMA((picks,)),
        ],
        compiler_params=pltpu.CompilerParams(vmem_limit_bytes=8 << 20),
        cost_estimate=pl.CostEstimate(
            flops=0, bytes_accessed=4 * picks * size * width, transcendentals=0
        ),
        name="pick_blocks",
    )(incoming, *pieces)


def layer_kernel(
    dense, table, weight, cotangent, activ, grads,
    d_buf, act_buf, grad_buf, wgrad, row_grad, d_sem, act_sem, grad_sem,
):
    rows, cols = dense.shape
    peers, _, size = grads.shape
    width = weight.shape[0]
    steps = act_sem.shape[0]
    row_step = rows // steps
    col_step = cols // grad_sem.shape[0]
    per_peer = cols // size // peers
    peers_done = col_step // size // per_peer

    def fetch(i):
        part = block(i, row_step)
        return pltpu.make_async_copy(dense.at[part], d_buf.at[part], d_sem.at[i])

    def put_activ(i):
        part = block(i, row_step)
        return pltpu.make_async_copy(act_buf.at[part], activ.at[part], act_sem.at[i])

    def put_grads(j):
        part = pl.ds(j * peers_done, peers_done)
        return pltpu.make_async_copy(grad_buf.at[part], grads.at[part], grad_sem.at[j])

    for i in range(steps):
        fetch(i).start()
    wgrad[...] = jnp.zeros_like(wgrad)

    def forward(i, _):
        fetch(i).wait()
        part = block(i, row_step)
        agg = jnp.dot(d_buf[part, :], table[...], preferred_element_type=jnp.float32)
        agg = agg.astype(jnp.bfloat16)
        w = weight[...]
        pre = jnp.dot(agg, w, preferred_element_type=jnp.float32)
        square = pre * pre
        tanh = jnp.tanh(pre * (GELU_SCALE + (GELU_SCALE * GELU_CUBE) * square))
        half = 0.5 + 0.5 * tanh
        act_buf[part, :] = (pre * half).astype(jnp.bfloat16)
        bend = 0.5 * GELU_SCALE + (1.5 * GELU_SCALE * GELU_CUBE) * square
        slope = half + (pre - pre * (tanh * tanh)) * bend
        pre_grad = (cotangent[part, :].astype(jnp.float32) * slope).astype(jnp.bfloat16)
        wgrad[...] += lax.dot_general(
            agg, pre_grad, (((0,), (0,)), ((), ())), preferred_element_type=jnp.float32
        )
        row_grad[:, part] = lax.dot_general(
            w, pre_grad, (((1,), (1,)), ((), ())), preferred_element_type=jnp.float32
        ).astype(jnp.bfloat16)
        put_activ(i).start()
        return 0

    lax.fori_loop(0, steps, forward, 0)

    strip = width // peers
    for p in range(peers):
        rows_of_p = wgrad[p * strip : (p + 1) * strip, :].astype(jnp.bfloat16)
        for q in range(width // size):
            at = per_peer * width + q * strip
            grad_buf[p, at : at + strip] = rows_of_p[:, q * size : (q + 1) * size]

    def backward(j, _):
        grad = jnp.dot(
            row_grad[...], d_buf[:, block(j, col_step)], preferred_element_type=jnp.float32
        ).astype(jnp.bfloat16)
        for p in range(peers_done):
            for q in range(per_peer):
                at = (p * per_peer + q) * size
                grad_buf[j * peers_done + p, q * width : (q + 1) * width] = grad[:, at : at + size]
        put_grads(j).start()
        return 0

    lax.fori_loop(0, cols // col_step, backward, 0)
    for i in range(steps):
        put_activ(i).wait()
    for j in range(cols // col_step):
        put_grads(j).wait()


def layer(dense, table, weight, cotangent, size, peers):
    rows, cols = dense.shape
    width = weight.shape[0]
    sent_rows = cols // size // peers * width + width // peers * (width // size)
    row_step, col_step = 4 * size, 16 * size
    grads = jax.ShapeDtypeStruct((peers, sent_rows, size), jnp.bfloat16)
    return pl.pallas_call(
        layer_kernel,
        out_shape=(jax.ShapeDtypeStruct(cotangent.shape, jnp.bfloat16), grads),
        in_specs=[ANY, VMEM, VMEM, VMEM],
        out_specs=(ANY, ANY),
        scratch_shapes=[
            pltpu.VMEM(dense.shape, jnp.bfloat16),
            pltpu.VMEM(cotangent.shape, jnp.bfloat16),
            pltpu.VMEM(grads.shape, jnp.bfloat16),
            pltpu.VMEM((width, width), jnp.float32),
            pltpu.VMEM((width, rows), jnp.bfloat16),
            pltpu.SemaphoreType.DMA((rows // row_step,)),
            pltpu.SemaphoreType.DMA((rows // row_step,)),
            pltpu.SemaphoreType.DMA((cols // col_step,)),
        ],
        compiler_params=pltpu.CompilerParams(vmem_limit_bytes=40 << 20),
        cost_estimate=pl.CostEstimate(
            flops=4 * rows * cols * width, bytes_accessed=2 * dense.size, transcendentals=0
        ),
        name="layer",
    )(dense, table, weight, cotangent)


def group_sums_kernel(incoming, returned, keep, send, total):
    half, width, _ = keep.shape
    peers, per_peer = incoming.shape
    row = lax.axis_index("row")
    chips = lax.axis_size("row") // 2
    total[...] = jnp.zeros_like(total)

    def add(peer, _):
        for j in range(per_peer):
            wanted = incoming[peer, j]

            @pl.when(wanted >= 0)
            def _():
                at = block_place(jnp.maximum(wanted, 0), row, chips, half // chips, True)
                total[at] += returned[peer, j * width : (j + 1) * width].astype(jnp.float32)

        return 0

    lax.fori_loop(0, peers, add, 0)
    keep[...] = total[:half]
    send[...] = total[half:].astype(jnp.bfloat16)


def group_sums(incoming, returned, groups, width):
    size = returned.shape[2]
    half = (groups // 2, width, size)
    return pl.pallas_call(
        group_sums_kernel,
        out_shape=(
            jax.ShapeDtypeStruct(half, jnp.float32),
            jax.ShapeDtypeStruct(half, jnp.bfloat16),
        ),
        in_specs=[SMEM, VMEM],
        out_specs=(VMEM, VMEM),
        scratch_shapes=[pltpu.VMEM((groups, width, size), jnp.float32)],
        compiler_params=pltpu.CompilerParams(vmem_limit_bytes=16 << 20),
        cost_estimate=pl.CostEstimate(
            flops=returned.size, bytes_accessed=4 * returned.size, transcendentals=0
        ),
        name="group_sums",
    )(incoming, returned)


def chip_sums_kernel(keep, arrived, own, *messages):
    panels = own.shape[0]
    for d in range(1 + len(messages)):
        for p in range(panels):
            total = keep[d * panels + p] + arrived[d * panels + p].astype(jnp.float32)
            if d == 0:
                own[p] = total
            else:
                messages[d - 1][p] = total.astype(jnp.bfloat16)


def chip_sums(keep, arrived, chips):
    half, width, size = keep.shape
    each = (half // chips, width, size)
    shapes = [jax.ShapeDtypeStruct(each, jnp.float32)]
    shapes += [jax.ShapeDtypeStruct(each, jnp.bfloat16)] * (chips - 1)
    return pl.pallas_call(
        chip_sums_kernel,
        out_shape=shapes,
        in_specs=[VMEM] * 2,
        out_specs=[VMEM] * chips,
        compiler_params=pltpu.CompilerParams(vmem_limit_bytes=8 << 20),
        cost_estimate=pl.CostEstimate(flops=keep.size, bytes_accessed=8 * keep.size, transcendentals=0),
        name="chip_sums",
    )(keep, arrived)


def owner_sum_kernel(own, *refs):
    parts, out = refs[:-1], refs[-1]
    for p in range(out.shape[0]):
        total = own[p]
        for part in parts:
            total = total + part[p].astype(jnp.float32)
        out[p] = total.T.astype(jnp.bfloat16)


def owner_sum(own, parts):
    panels, width, size = own.shape
    return pl.pallas_call(
        owner_sum_kernel,
        out_shape=jax.ShapeDtypeStruct((panels, size, width), jnp.bfloat16),
        in_specs=[VMEM] * (1 + len(parts)),
        out_specs=VMEM,
        compiler_params=pltpu.CompilerParams(vmem_limit_bytes=8 << 20),
        cost_estimate=pl.CostEstimate(flops=own.size, bytes_accessed=8 * own.size, transcendentals=0),
        name="owner_sum",
    )(own, *parts)


def local(features, adjacency, requests, block_coords, weight, cotangent):
    panels, span, width = features.shape
    size = adjacency.shape[-1]
    grid_rows = lax.axis_size("row")
    grid_cols = lax.axis_size("col")
    chips = grid_rows // 2
    out_blocks = cotangent.shape[0] // size
    wanted = requests[0, 0]
    per_peer = wanted.shape[1]
    slots = grid_cols * per_peer

    def exchange(values, axis):
        return lax.all_to_all(values, axis, split_axis=0, concat_axis=0, tiled=True)

    def to_other_core(values):
        return lax.ppermute(values, "row", [(r, r ^ 1) for r in range(grid_rows)])

    def to_chip_ahead(values, ahead):
        return lax.ppermute(
            values, "row", [(r, (r + 2 * ahead) % grid_rows) for r in range(grid_rows)]
        )

    incoming = exchange(wanted, "col")
    mine = [features] + [to_chip_ahead(features, d) for d in range(1, chips)]
    incoming, mine[2] = lax.optimization_barrier((incoming, mine[2]))
    pieces = mine + [to_other_core(piece) for piece in mine]
    sends = pick_blocks(incoming, pieces)

    coords = block_coords[0, 0]
    lists = cell_lists(coords[:, 0], coords[:, 1], out_blocks, slots)
    edges = adjacency[0, 0]
    dense = densify(lists, edges, out_blocks, slots, 1)
    sends, dense = lax.optimization_barrier((sends, dense))
    table = exchange(sends, "col").reshape(slots * size, width)
    dense = densify(lists, edges, out_blocks, slots, 0, (dense,))

    activations, grads = layer(dense, table, weight, cotangent, size, grid_cols)

    returned = exchange(grads, "col")
    strip = jnp.sum(returned[:, per_peer * width :].astype(jnp.float32), axis=0)

    strip = strip + to_other_core(strip)
    near = [strip] + [to_chip_ahead(strip, d) for d in range(1, chips)]
    strip = sum(near[2::2], near[0]) + sum(near[3::2], near[1])

    keep, send = group_sums(incoming, returned, panels * grid_rows, width)
    own, *messages = chip_sums(keep, to_other_core(send), chips)
    strip, *messages = lax.optimization_barrier((strip, *messages))
    parts = [to_chip_ahead(message, d + 1) for d, message in enumerate(messages)]

    copies = jnp.broadcast_to(strip.astype(jnp.bfloat16)[None], (grid_cols, *strip.shape))
    strips = exchange(copies, "col").reshape(grid_cols, width // size, width // grid_cols, size)
    weight_grad = jnp.swapaxes(strips, 1, 2).reshape(width, width).astype(jnp.float32)
    own, weight_grad = lax.optimization_barrier((own, weight_grad))
    feature_grad = owner_sum(own, parts)
    return (activations, weight_grad, feature_grad)


def solution(mesh):
    placed = (
        P(None, ("row", "col"), None),
        P("row", "col", None, None, None),
        P("row", "col", None, None),
        P("row", "col", None, None),
        P(),
        P(("row", "col"), None),
    )
    return jax.shard_map(
        local,
        mesh=mesh,
        in_specs=placed,
        out_specs=(P(("row", "col"), None), P(), P(None, ("row", "col"), None)),
        check_vma=False,
    )
```
